1024 devices in a mesh: row: 8 (over z), col: 16 (over y, x_lo), layer: 8 (over x_hi, core).
Axes of the slice: x: 8 (x_hi: 4, x_lo: 2; x = x_hi * 2 + x_lo), y: 8, z: 8, core: 2. Of those that a mesh axis runs over, the one named last changes fastest.
Arguments:
- stored: bfloat16 [8192, 8192], P(('row', 'layer')), may hold values from -0.5 to 0.5
- pattern: int32 [64, 64], replicated, may hold values 0 or 1
Outputs:
- density_square: bfloat16 [8192, 8192], P(('row', 'layer'), 'col')
The draws below stay inside these ranges and needn't reach their ends.
All inputs are finite; a program needn't handle non-finite values.
Results may differ from the reference program's by a relative error of at most 0.0011.
Values may be sent and summed in bfloat16 or wider, within the bound.
No kernel may reach another device: no remote copies, remote signals or barrier semaphores. Data moves between devices by JAX's collectives and lax.ppermute only.
A program may use at most 32 MiB of HBM per device.

```python
import jax
import jax.numpy as jnp
from jax import lax

BS = 128
NB = 64
NW = 8192


def plant(values, rng, smallest, largest):
    longest = values.shape.index(max(values.shape))
    spots = []
    for shift in (0, 1):
        where = [jax.random.randint(jax.random.fold_in(rng, axis), (), 0, length) for axis, length in enumerate(values.shape)]
        where[longest] = (where[longest] + shift) % values.shape[longest]
        spots.append(tuple(where))
    return values.at[spots[0]].set(smallest).at[spots[1]].set(largest)


def level_of(own_key, extent, pieces, low, largest):
    def one(dim, parts):
        draws = jax.random.uniform(jax.random.fold_in(jax.random.fold_in(own_key, 6), dim), (parts,), jnp.float32, low / len(pieces), largest / len(pieces))
        return jnp.repeat(jnp.exp(draws), extent[dim] // parts).reshape((-1,) + (1,) * (len(extent) - dim - 1))

    gain = one(*pieces[0])
    for cut in pieces[1:]:
        gain = gain * one(*cut)
    return gain


def normal_values(stream_key, shape, spread, most, cuts=(), held_as=jnp.bfloat16):
    values = spread * jax.random.normal(stream_key, shape, jnp.float32)
    if cuts:
        values = values * level_of(stream_key, shape, cuts, -0.22, 0.18)
    return jnp.clip(values, -most, most).astype(held_as)


def setup_inputs(seed: int = 0) -> dict:
    seeds = jax.random.split(jax.random.key(seed), 3)
    return {
        "stored": normal_values(seeds[0], (NW, NW), (NW // 64) ** -0.5, 0.5, ((0, 64),)),
        "pattern": plant((jax.random.randint(seeds[1], (NB, NB), 0, 2) < 1).astype(jnp.int32), jax.random.fold_in(seeds[1], 1), 0, 1),
    }


def mirrored_rows(stored, pattern, block_index):
    full_width = stored.shape[1]
    own_rows = lax.dynamic_slice_in_dim(stored, block_index * BS, BS, 0)
    column_strip = lax.dynamic_slice_in_dim(stored, block_index * BS, BS, 1).T
    row_pattern = jnp.repeat(lax.dynamic_index_in_dim(pattern, block_index, 0, keepdims=False), BS)
    column_pattern = jnp.repeat(lax.dynamic_index_in_dim(pattern, block_index, 1, keepdims=False), BS)
    row_index = block_index * BS + jnp.arange(BS, dtype=jnp.int32)[:, None]
    column_index = jnp.arange(full_width, dtype=jnp.int32)[None, :]
    nothing = jnp.zeros_like(own_rows)
    upper_part = jnp.where(row_pattern[None, :] > 0, own_rows, nothing)
    lower_part = jnp.where(column_pattern[None, :] > 0, column_strip, nothing)
    return jnp.where(column_index >= row_index, upper_part, lower_part)


def reference(stored, pattern):
    def one_block(block_index):
        return mirrored_rows(stored, pattern, block_index)

    blocks = lax.map(one_block, jnp.arange(NB, dtype=jnp.int32))
    density = blocks.reshape(NW, NW).astype(jnp.float32)
    square = jnp.dot(density, density, precision=lax.Precision.HIGHEST, preferred_element_type=jnp.float32)
    return square.astype(jnp.bfloat16)
```

```python
import jax
import jax.numpy as jnp
from jax import lax
from jax.sharding import PartitionSpec as P

B = 128


def body(stored, pattern):
    rows, width = stored.shape
    nz = lax.axis_size("row")
    nl = lax.axis_size("layer")
    nc = lax.axis_size("col")
    z = lax.axis_index("row")
    l = lax.axis_index("layer")
    c = lax.axis_index("col")
    g = z * nl + l
    plane = width // nz
    panel = width // nc
    per = panel // B
    half = nl // per

    row_pattern = lax.dynamic_index_in_dim(pattern, g, 0, keepdims=False)
    row_position = g * B + jnp.arange(B, dtype=jnp.int32)[:, None]
    column_position = jnp.arange(width, dtype=jnp.int32)[None, :]
    present = jnp.repeat(row_pattern, B)[None, :] > 0
    zero = jnp.zeros((), stored.dtype)
    upper = jnp.where(present & (column_position >= row_position), stored, zero)
    strict = jnp.where(present & (column_position > row_position), stored, zero)

    def flat(zz, cc, ll):
        return (zz * nc + cc) * nl + ll

    received = []
    for s in range(per):
        pairs = []
        for zz in range(nz):
            for cc in range(nc):
                for ll in range(nl):
                    a = zz * nl + ll
                    t = cc * per + (ll % per + s) % per
                    if a <= t:
                        pairs.append((flat(zz, cc, ll), flat(t // nl, a // per, t % nl)))
        j = (l % per + s) % per
        block = lax.dynamic_slice(upper, (0, (c * per + j) * B), (B, B))
        received.append(lax.ppermute(block, ("row", "col", "layer"), pairs))
    ordered = jnp.concatenate(received[::-1] + received[::-1][:-1], axis=0)
    ordered = lax.dynamic_slice(ordered, (((per - 1 - l) % per) * B, 0), (panel, B))
    tile_column = c * panel + jnp.arange(panel, dtype=jnp.int32)[None, :]
    tile = lax.dynamic_slice(upper, (0, c * panel), (B, panel))
    tile = jnp.where(tile_column >= row_position, tile, ordered.T)

    lower = []
    right = []
    for s in range(nz):
        shift = (nz - s) % nz
        target = lax.rem(z + shift, nz)
        piece = lax.dynamic_slice(upper, (0, target * plane), (B, plane))
        if shift:
            piece = lax.ppermute(piece, "row", [(k, k + shift) for k in range(nz - shift)])
        lower.append(piece)
        right.append(tile if not shift else lax.ppermute(tile, "row", [(k, (k + shift) % nz) for k in range(nz)]))
    lower = jnp.concatenate(lower, axis=0)
    right = jnp.concatenate(right, axis=0)

    rolled = lax.dynamic_slice(jnp.concatenate([strict, strict], axis=1), (0, z * plane), (B, width))
    rolled = rolled.reshape(B, nz, nl, B).transpose(2, 0, 1, 3)
    high = lax.all_to_all(rolled, "layer", split_axis=0, concat_axis=0, tiled=True)
    high = high.reshape(nl * B, nz * B)

    partial = lax.dot_general(
        lower, right, (((0,), (0,)), ((), ())), preferred_element_type=jnp.float32
    ) + jnp.dot(high, right, preferred_element_type=jnp.float32)
    parts = lax.all_to_all(partial.reshape(nl, B, panel), "layer", split_axis=0, concat_axis=0, tiled=True)
    return jnp.sum(parts, axis=0).astype(jnp.bfloat16)


def solution(mesh):
    return jax.shard_map(
        body,
        mesh=mesh,
        in_specs=(P(("row", "layer"), None), P()),
        out_specs=P(("row", "layer"), "col"),
        check_vma=False,
    )
```

```python
import jax
import jax.numpy as jnp
from jax import lax
from jax.sharding import Mesh, PartitionSpec as P

B = 128
AXES = ("z", "y", "w", "u", "v", "core")


def body(stored, pattern):
    nz, ny, nw, nu, nv, ncore = (lax.axis_size(a) for a in AXES)
    z, y, w, u, v, core = (lax.axis_index(a) for a in AXES)
    four = nv * ncore
    wide = four * B
    i = v * ncore + core
    ra = z * nu + u
    c = y * nw + w
    g = ra * four + i

    band = nw * wide
    raw = lax.dynamic_slice(stored, (0, y * band), (B, band))
    present = lax.dynamic_slice(pattern, (g, y * nw * four), (1, nw * four))
    present = jnp.repeat(present, B, axis=1) > 0
    row = g * B + jnp.arange(B, dtype=jnp.int32)[:, None]
    column = y * band + jnp.arange(band, dtype=jnp.int32)[None, :]
    upper = jnp.where(present & (column >= row), raw, jnp.zeros((), raw.dtype))
    tile = lax.dynamic_slice(upper, (0, w * wide), (B, wide))

    def flat(zz, uu, yy, ww, ii):
        return (((zz * ny + yy) * nw + ww) * nu + uu) * four + ii

    everywhere = [
        (zz, uu, yy, ww, ii)
        for zz in range(nz)
        for uu in range(nu)
        for yy in range(ny)
        for ww in range(nw)
        for ii in range(four)
    ]

    blocks = tile.reshape(B, four, B).transpose(1, 0, 2)
    crossed = lax.all_to_all(blocks, ("v", "core"), split_axis=0, concat_axis=0, tiled=True)
    crossed = crossed.reshape(wide, B).T
    mirrored = lax.ppermute(
        tile,
        AXES,
        [(flat(*d), flat(d[2], d[3], d[0], d[1], d[4])) for d in everywhere if d[0] * nu + d[1] <= d[2] * nw + d[3]],
    )
    k_row = (c * four + i) * B + jnp.arange(B, dtype=jnp.int32)[:, None]
    i_column = ra * wide + jnp.arange(wide, dtype=jnp.int32)[None, :]
    left = jnp.where(k_row <= i_column, mirrored, crossed)

    received = []
    for s in range(four):
        j = (i + s) % four
        pair = jnp.concatenate(
            [lax.dynamic_slice(upper, (0, (h * four + j) * B), (B, B)) for h in range(nw)], axis=1
        )
        received.append(
            lax.ppermute(
                pair,
                AXES,
                [
                    (flat(*d), flat(d[2], d[3], d[0], d[1], (d[4] + s) % four))
                    for d in everywhere
                    if d[0] * nu + d[1] <= d[2] * nw + nw - 1
                ],
            )
        )
    backward = received[::-1]
    ring = jnp.stack(backward + backward[:-1])
    ring = lax.dynamic_slice(ring, ((four - 1 - i) % four, 0, 0), (four, B, nu * B))
    turned = ring.reshape(wide, nu * B).T
    other = lax.ppermute(tile, "u", [(a, nu - 1 - a) for a in range(nu)])
    first = u == 0
    direct = jnp.concatenate([jnp.where(first, tile, other), jnp.where(first, other, tile)], axis=0)
    half = jnp.arange(nu, dtype=jnp.int32)[:, None]
    r_row = ((z * nu + half) * four + i) * B + jnp.arange(B, dtype=jnp.int32)[None, :]
    r_row = r_row.reshape(nu * B, 1)
    j_column = c * wide + jnp.arange(wide, dtype=jnp.int32)[None, :]
    right = jnp.where(r_row <= j_column, direct, turned)

    right = lax.all_gather(right, "z", axis=0, tiled=True)
    left = jnp.broadcast_to(left[None], (ny * nw, B, wide))
    left = lax.all_to_all(left, ("y", "w"), split_axis=0, concat_axis=0, tiled=True)
    left = left.reshape(ny * nw * B, wide)

    partial = lax.dot_general(left, right, (((0,), (0,)), ((), ())), preferred_element_type=jnp.float32)
    partial = partial.reshape(nv, ncore, B, wide)
    partial = jnp.sum(lax.all_to_all(partial, "core", split_axis=1, concat_axis=1, tiled=True), axis=1)
    partial = jnp.sum(lax.all_to_all(partial, "v", split_axis=0, concat_axis=0, tiled=True), axis=0)
    return partial.astype(jnp.bfloat16)


def solution(mesh):
    finer = Mesh(mesh.devices.reshape(8, 8, 2, 2, 2, 2), AXES)
    return jax.shard_map(
        body,
        mesh=finer,
        in_specs=(P(("z", "u", "v", "core"), None), P()),
        out_specs=P(("z", "u", "v", "core"), ("y", "w")),
        check_vma=False,
    )
```

```python
import jax
import jax.numpy as jnp
from jax import lax
from jax.experimental import pallas as pl
from jax.experimental.pallas import tpu as pltpu
from jax.sharding import Mesh, PartitionSpec as P

B = 128
AXES = ("z", "y", "w", "u", "v", "core")


def product_kernel(left_ref, right_ref, out_ref):
    pieces = [left_ref[k] for k in range(left_ref.shape[0])]
    out_ref[...] = jnp.dot(jnp.concatenate(pieces, axis=1), right_ref[...], preferred_element_type=jnp.float32)


def product(left, right, swap):
    count, rows, depth = left.shape
    columns = right.shape[1]
    step = B
    return pl.pallas_call(
        product_kernel,
        grid=(rows // step,),
        in_specs=[
            pl.BlockSpec((count, step, depth), lambda m: (0, m, 0)),
            pl.BlockSpec((count * depth, columns), lambda m: (0, 0)),
        ],
        out_specs=pl.BlockSpec((step, columns), lambda m: ((m % swap) * (rows // step // swap) + m // swap, 0)),
        out_shape=jax.ShapeDtypeStruct((rows, columns), jnp.float32),
        compiler_params=pltpu.CompilerParams(vmem_limit_bytes=24 * 1024 * 1024),
        cost_estimate=pl.CostEstimate(
            flops=2 * rows * columns * count * depth,
            bytes_accessed=2 * (left.size + right.size) + 4 * rows * columns,
            transcendentals=0,
        ),
        name="product",
    )(left, right)


def body(stored, pattern):
    nz, ny, nw, nu, nv, ncore = (lax.axis_size(a) for a in AXES)
    z, y, w, u, v, core = (lax.axis_index(a) for a in AXES)
    four = nv * ncore
    wide = four * B
    i = v * ncore + core
    ra = z * nu + u
    c = y * nw + w
    g = ra * four + i

    raw = lax.dynamic_slice(stored, (0, c * wide), (B, wide))
    present = lax.dynamic_slice(pattern, (g, c * four), (1, four))
    present = jnp.repeat(present, B, axis=1) > 0
    row = g * B + jnp.arange(B, dtype=jnp.int32)[:, None]
    column = c * wide + jnp.arange(wide, dtype=jnp.int32)[None, :]
    tile = jnp.where(present & (column >= row), raw, jnp.zeros((), raw.dtype))

    def flat(zz, uu, yy, ww, ii):
        return (((zz * ny + yy) * nw + ww) * nu + uu) * four + ii

    everywhere = [
        (zz, uu, yy, ww, ii)
        for zz in range(nz)
        for uu in range(nu)
        for yy in range(ny)
        for ww in range(nw)
        for ii in range(four)
    ]

    mirrored = lax.ppermute(
        tile,
        AXES,
        [(flat(*d), flat(d[2], d[3], d[0], d[1], d[4])) for d in everywhere if d[0] * nu + d[1] < d[2] * nw + d[3]],
    )
    other = lax.ppermute(tile, "u", [(a, nu - 1 - a) for a in range(nu)])
    own = jnp.where(ra <= c, tile, mirrored)
    blocks = own.reshape(B, four, B).transpose(1, 0, 2)
    blocks = jnp.concatenate([blocks] * nu, axis=0)
    crossed = lax.all_to_all(blocks, ("u", "v", "core"), split_axis=0, concat_axis=0, tiled=True)
    crossed = crossed.reshape(nu, wide, B)

    first = u == 0
    i_row = ra * wide + jnp.arange(wide, dtype=jnp.int32)[:, None]
    k_column = (c * four + i) * B + jnp.arange(B, dtype=jnp.int32)[None, :]
    left = jnp.where(k_column <= i_row, own.T, jnp.where(first, crossed[0], crossed[1]))

    direct = jnp.stack([jnp.where(first, tile, other), jnp.where(first, other, tile)])
    half = jnp.arange(nu, dtype=jnp.int32)[:, None, None]
    r_row = ((z * nu + half) * four + i) * B + jnp.arange(B, dtype=jnp.int32)[None, :, None]
    j_column = c * wide + jnp.arange(wide, dtype=jnp.int32)[None, None, :]
    right = jnp.where(r_row <= j_column, direct, crossed.transpose(0, 2, 1)).reshape(nu * B, wide)

    left, right = lax.optimization_barrier((left, right))
    right = lax.all_gather(right, "z", axis=0, tiled=True)
    left = jnp.broadcast_to(left[None], (ny * nw, wide, B))
    left = lax.all_to_all(left, ("y", "w"), split_axis=0, concat_axis=0, tiled=True)
    partial = product(left, right, ncore)
    partial = partial.reshape(ncore, nv, B, wide)
    partial = jnp.sum(lax.all_to_all(partial, "core", split_axis=0, concat_axis=0, tiled=True), axis=0)
    partial = jnp.sum(lax.all_to_all(partial, "v", split_axis=0, concat_axis=0, tiled=True), axis=0)
    return partial.astype(jnp.bfloat16)


def solution(mesh):
    finer = Mesh(mesh.devices.reshape(8, 8, 2, 2, 2, 2), AXES)
    return jax.shard_map(
        body,
        mesh=finer,
        in_specs=(P(("z", "u", "v", "core"), None), P()),
        out_specs=P(("z", "u", "v", "core"), ("y", "w")),
        check_vma=False,
    )
```

```python
import jax
import jax.numpy as jnp
from jax import lax
from jax.experimental import pallas as pl
from jax.experimental.pallas import tpu as pltpu
from jax.sharding import Mesh, PartitionSpec as P

B = 128
AXES = ("z", "y", "w", "u", "v", "core")


def first_rows_kernel(right_ref, out_ref):
    out_ref[...] = right_ref[...]


def first_rows(right):
    shape = (16, right.shape[1])
    return pl.pallas_call(
        first_rows_kernel,
        grid=(1,),
        in_specs=[pl.BlockSpec(shape, lambda m: (0, 0))],
        out_specs=pl.BlockSpec(shape, lambda m: (0, 0)),
        out_shape=jax.ShapeDtypeStruct(shape, right.dtype),
        cost_estimate=pl.CostEstimate(flops=10**11, bytes_accessed=10**8, transcendentals=0),
        name="first_rows",
    )(right)


def product_kernel(left_ref, right_ref, rows_ref, out_ref):
    pieces = [left_ref[k] for k in range(left_ref.shape[0])]
    out_ref[...] = jnp.dot(jnp.concatenate(pieces, axis=1), right_ref[...], preferred_element_type=jnp.float32)


def product(left, right, swap):
    count, rows, depth = left.shape
    columns = right.shape[1]
    step = B
    return pl.pallas_call(
        product_kernel,
        grid=(rows // step,),
        in_specs=[
            pl.BlockSpec((count, step, depth), lambda m: (0, m, 0)),
            pl.BlockSpec((count * depth, columns), lambda m: (0, 0)),
            pl.BlockSpec((16, columns), lambda m: (0, 0)),
        ],
        out_specs=pl.BlockSpec((step, columns), lambda m: ((m % swap) * (rows // step // swap) + m // swap, 0)),
        out_shape=jax.ShapeDtypeStruct((rows, columns), jnp.float32),
        compiler_params=pltpu.CompilerParams(vmem_limit_bytes=24 * 1024 * 1024),
        cost_estimate=pl.CostEstimate(
            flops=2 * rows * columns * count * depth,
            bytes_accessed=2 * (left.size + right.size) + 4 * rows * columns,
            transcendentals=0,
        ),
        name="product",
    )(left, right, first_rows(right))


def body(stored, pattern):
    nz, ny, nw, nu, nv, ncore = (lax.axis_size(a) for a in AXES)
    z, y, w, u, v, core = (lax.axis_index(a) for a in AXES)
    four = nv * ncore
    wide = four * B
    i = v * ncore + core
    ra = z * nu + u
    c = y * nw + w
    g = ra * four + i

    raw = lax.dynamic_slice(stored, (0, c * wide), (B, wide))
    present = lax.dynamic_slice(pattern, (g, c * four), (1, four))
    present = jnp.repeat(present, B, axis=1) > 0
    row = g * B + jnp.arange(B, dtype=jnp.int32)[:, None]
    column = c * wide + jnp.arange(wide, dtype=jnp.int32)[None, :]
    tile = jnp.where(present & (column >= row), raw, jnp.zeros((), raw.dtype))

    def flat(zz, uu, yy, ww, ii):
        return (((zz * ny + yy) * nw + ww) * nu + uu) * four + ii

    everywhere = [
        (zz, uu, yy, ww, ii)
        for zz in range(nz)
        for uu in range(nu)
        for yy in range(ny)
        for ww in range(nw)
        for ii in range(four)
    ]

    mirrored = lax.ppermute(
        tile,
        AXES,
        [(flat(*d), flat(d[2], d[3], d[0], d[1], d[4])) for d in everywhere if d[0] * nu + d[1] < d[2] * nw + d[3]],
    )
    mirrored, later = lax.optimization_barrier((mirrored, tile))
    other = lax.ppermute(later, "u", [(a, nu - 1 - a) for a in range(nu)])
    own = jnp.where(ra <= c, tile, mirrored)
    blocks = own.reshape(B, four, B).transpose(1, 0, 2)
    blocks = jnp.concatenate([blocks] * nu, axis=0)
    crossed = lax.all_to_all(blocks, ("u", "v", "core"), split_axis=0, concat_axis=0, tiled=True)
    crossed, other, plain = lax.optimization_barrier((crossed, other, tile))
    crossed = crossed.reshape(nu, wide, B)

    first = u == 0
    i_row = ra * wide + jnp.arange(wide, dtype=jnp.int32)[:, None]
    k_column = (c * four + i) * B + jnp.arange(B, dtype=jnp.int32)[None, :]
    left = jnp.where(k_column <= i_row, own.T, jnp.where(first, crossed[0], crossed[1]))

    direct = jnp.stack([jnp.where(first, plain, other), jnp.where(first, other, plain)])
    half = jnp.arange(nu, dtype=jnp.int32)[:, None, None]
    r_row = ((z * nu + half) * four + i) * B + jnp.arange(B, dtype=jnp.int32)[None, :, None]
    j_column = c * wide + jnp.arange(wide, dtype=jnp.int32)[None, None, :]
    right = jnp.where(r_row <= j_column, direct, crossed.transpose(0, 2, 1)).reshape(nu * B, wide)

    left, right = lax.optimization_barrier((left, right))
    right = lax.all_gather(right, "z", axis=0, tiled=True)
    left = jnp.broadcast_to(left[None], (ny * nw, wide, B))
    left = lax.all_to_all(left, ("y", "w"), split_axis=0, concat_axis=0, tiled=True)
    partial = product(left, right, ncore)
    partial = partial.reshape(ncore, nv, B, wide)
    partial = jnp.sum(lax.all_to_all(partial, "core", split_axis=0, concat_axis=0, tiled=True), axis=0)
    partial = jnp.sum(lax.all_to_all(partial, "v", split_axis=0, concat_axis=0, tiled=True), axis=0)
    return partial.astype(jnp.bfloat16)


def solution(mesh):
    finer = Mesh(mesh.devices.reshape(8, 8, 2, 2, 2, 2), AXES)
    return jax.shard_map(
        body,
        mesh=finer,
        in_specs=(P(("z", "u", "v", "core"), None), P()),
        out_specs=P(("z", "u", "v", "core"), ("y", "w")),
        check_vma=False,
    )
```

```python
import jax
import jax.numpy as jnp
from jax import lax
from jax.experimental import pallas as pl
from jax.experimental.pallas import tpu as pltpu
from jax.sharding import Mesh, PartitionSpec as P

B = 128
AXES = ("z", "y", "w", "u", "v", "core")
TAIL = 16


def product_kernel(y_ref, *refs):
    *left_refs, right_ref, out_ref, ordered = refs
    n, depth, _ = right_ref.shape
    y = y_ref[0]

    @pl.when(pl.program_id(0) == 0)
    def _():
        for s in range(n):
            ordered[s * depth : (s + 1) * depth, :] = right_ref[lax.rem(y - s + n, n)]

    left = jnp.concatenate([r[...] for r in left_refs], axis=0)
    total = lax.dot_general(
        left, ordered[...], (((0,), (0,)), ((), ())), preferred_element_type=jnp.float32
    )
    cores, ways, rows, columns = out_ref.shape
    for a in range(cores):
        for b in range(ways):
            out_ref[a, b] = total[a * rows : (a + 1) * rows, b * columns : (b + 1) * columns]


def product(lefts, right, y, cores, ways):
    n, depth, wide = right.shape
    step = cores * B
    panel = wide // ways
    return pl.pallas_call(
        product_kernel,
        grid_spec=pltpu.PrefetchScalarGridSpec(
            num_scalar_prefetch=1,
            grid=(wide // step,),
            in_specs=[pl.BlockSpec((depth, step), lambda m, _: (0, m)) for _ in lefts]
            + [pl.BlockSpec((n, depth, wide), lambda m, _: (0, 0, 0))],
            out_specs=pl.BlockSpec((cores, ways, B, panel), lambda m, _: (0, m, 0, 0)),
            scratch_shapes=[pltpu.VMEM((n * depth, wide), right.dtype)],
        ),
        out_shape=jax.ShapeDtypeStruct((cores, wide // step * ways, B, panel), jnp.float32),
        compiler_params=pltpu.CompilerParams(vmem_limit_bytes=24 * 1024 * 1024),
        cost_estimate=pl.CostEstimate(
            flops=2 * n * depth * wide * wide,
            bytes_accessed=4 * n * depth * wide + 4 * wide * wide,
            transcendentals=0,
        ),
        name="product",
    )(y.reshape(1), *lefts, right)


def body(stored, pattern):
    nz, ny, nw, nu, nv, ncore = (lax.axis_size(a) for a in AXES)
    z, y, w, u, v, core = (lax.axis_index(a) for a in AXES)
    nl = nu * nv * ncore
    l = (u * nv + v) * ncore + core
    g = z * nl + l
    plane = nl * B
    part = B // nw

    raw = lax.dynamic_slice(stored, (0, y * plane), (B, plane))
    present = lax.dynamic_slice(pattern, (g, y * nl), (1, nl))
    present = jnp.repeat(present, B, axis=1) > 0
    row = g * B + jnp.arange(B, dtype=jnp.int32)[:, None]
    column = y * plane + jnp.arange(plane, dtype=jnp.int32)[None, :]
    band = jnp.where(present & (column >= row), raw, jnp.zeros((), raw.dtype))

    def flat(zz, yy, r):
        return (zz * ny + yy) * (nw * nl) + r

    mirrored = lax.ppermute(
        band,
        AXES,
        [
            (flat(a, b, r), flat(b, a, r))
            for a in range(nz)
            for b in range(a + 1, ny)
            for r in range(nw * nl)
        ],
    )
    own = jnp.where(z <= y, band, mirrored)
    turned = own.T.reshape(nl, nw, part, B)
    turned = lax.dynamic_index_in_dim(turned, w, 1, keepdims=False)
    crossed = lax.all_to_all(turned, ("u", "v", "core"), split_axis=0, concat_axis=0, tiled=True)
    crossed = crossed.transpose(1, 0, 2).reshape(part, plane)
    straight = lax.dynamic_slice(own, (w * part, 0), (part, plane))

    offset = l * B + w * part + jnp.arange(part, dtype=jnp.int32)[:, None]
    across = jnp.arange(plane, dtype=jnp.int32)[None, :]
    left = jnp.where(y * plane + offset <= z * plane + across, straight, crossed)
    right = jnp.where(z * plane + offset <= y * plane + across, straight, crossed)

    right = jnp.broadcast_to(right[None], (nz, part, plane))
    right = lax.all_to_all(right, "z", split_axis=0, concat_axis=0, tiled=True)
    lefts = [left] + [lax.ppermute(left, "y", [(a, (a + s) % ny) for a in range(ny)]) for s in range(1, ny)]

    partial = product(lefts, right, y, ncore, nw)
    partial = jnp.sum(lax.all_to_all(partial, "core", split_axis=0, concat_axis=0, tiled=True), axis=0)

    most = jnp.max(jnp.abs(partial))
    power = jnp.clip(jnp.ceil(jnp.log2(jnp.maximum(most, 1e-30))) - 14.0, -100.0, 100.0)
    scaled = (partial * jnp.exp2(-power)).astype(jnp.float16)
    tail = jnp.broadcast_to(power.astype(jnp.float16), (scaled.shape[0], TAIL, scaled.shape[2]))
    sent = jnp.concatenate([scaled, tail], axis=1)
    got = lax.all_to_all(sent, ("u", "v", "w"), split_axis=0, concat_axis=0, tiled=True)
    scale = jnp.exp2(got[:, B, 0].astype(jnp.float32))
    total = jnp.sum(got[:, :B].astype(jnp.float32) * scale[:, None, None], axis=0)
    return total.astype(jnp.bfloat16)


def solution(mesh):
    finer = Mesh(mesh.devices.reshape(8, 8, 2, 2, 2, 2), AXES)
    return jax.shard_map(
        body,
        mesh=finer,
        in_specs=(P(("z", "u", "v", "core"), None), P()),
        out_specs=P(("z", "u", "v", "core"), ("y", "w")),
        check_vma=False,
    )
```

```python
import jax
import jax.numpy as jnp
from jax import lax
from jax.experimental import pallas as pl
from jax.experimental.pallas import tpu as pltpu
from jax.sharding import Mesh, PartitionSpec as P

B = 128
AXES = ("z", "y", "w", "u", "v", "core")


def product_kernel(z_ref, left_ref, *refs):
    *right_refs, out_ref, ordered = refs
    n, depth, step = left_ref.shape
    z = z_ref[0]

    @pl.when(pl.program_id(0) == 0)
    def _():
        for s, piece in enumerate(right_refs):
            ordered[lax.rem(z - s + n, n)] = piece[...]

    total = lax.dot_general(
        left_ref[...].reshape(n * depth, step),
        ordered[...].reshape(n * depth, ordered.shape[2]),
        (((0,), (0,)), ((), ())),
        preferred_element_type=jnp.float32,
    )
    for a in range(out_ref.shape[0]):
        out_ref[a, 0] = total[a * B : (a + 1) * B]


def product(left, rights, z, cores):
    n, depth, wide = left.shape
    panel = rights[0].shape[1]
    step = cores * B
    return pl.pallas_call(
        product_kernel,
        grid_spec=pltpu.PrefetchScalarGridSpec(
            num_scalar_prefetch=1,
            grid=(wide // step,),
            in_specs=[pl.BlockSpec((n, depth, step), lambda m, _: (0, 0, m))]
            + [pl.BlockSpec((depth, panel), lambda m, _: (0, 0)) for _ in rights],
            out_specs=pl.BlockSpec((cores, 1, B, panel), lambda m, _: (0, m, 0, 0)),
            scratch_shapes=[pltpu.VMEM((n, depth, panel), left.dtype)],
        ),
        out_shape=jax.ShapeDtypeStruct((cores, wide // step, B, panel), jnp.float32),
        compiler_params=pltpu.CompilerParams(vmem_limit_bytes=24 * 1024 * 1024),
        cost_estimate=pl.CostEstimate(
            flops=2 * n * depth * wide * panel,
            bytes_accessed=2 * n * depth * (wide + panel) + 4 * wide * panel,
            transcendentals=0,
        ),
        name="product",
    )(z.reshape(1), left, *rights)


def body(stored, pattern):
    nz, ny, nw, nu, nv, ncore = (lax.axis_size(a) for a in AXES)
    z, y, w, u, v, core = (lax.axis_index(a) for a in AXES)
    nl = nu * nv * ncore
    l = (u * nv + v) * ncore + core
    g = z * nl + l
    plane = nl * B
    panel = plane // nw

    raw = lax.dynamic_slice(stored, (0, y * plane), (B, plane))
    present = lax.dynamic_slice(pattern, (g, y * nl), (1, nl))
    present = jnp.repeat(present, B, axis=1) > 0
    row = g * B + jnp.arange(B, dtype=jnp.int32)[:, None]
    column = y * plane + jnp.arange(plane, dtype=jnp.int32)[None, :]
    band = jnp.where(present & (column >= row), raw, jnp.zeros((), raw.dtype))

    def flat(zz, yy, r):
        return (zz * ny + yy) * (nw * nl) + r

    mirror = [
        (flat(a, b, r), flat(b, a, r))
        for a in range(nz)
        for b in range(a + 1, ny)
        for r in range(nw * nl)
    ]

    turned = band.T.reshape(nl, B, B)
    crossed = lax.all_to_all(turned, ("u", "v", "core"), split_axis=0, concat_axis=0, tiled=True)
    crossed = crossed.transpose(1, 0, 2).reshape(B, plane)
    mirrored = lax.ppermute(band, AXES, mirror)
    half = lax.dynamic_slice(crossed, (0, w * panel), (B, panel))
    mirrored_half = lax.ppermute(half, AXES, mirror)

    diagonal = z == y
    offset = l * B + jnp.arange(B, dtype=jnp.int32)[:, None]
    across = jnp.arange(plane, dtype=jnp.int32)[None, :]
    left = jnp.where(
        y * plane + offset <= z * plane + across, jnp.where(diagonal, band, mirrored), crossed
    )
    own = y * plane + w * panel + jnp.arange(panel, dtype=jnp.int32)[None, :]
    right = jnp.where(
        z * plane + offset <= own,
        lax.dynamic_slice(band, (0, w * panel), (B, panel)),
        jnp.where(diagonal, half, mirrored_half),
    )

    left = jnp.broadcast_to(left[None], (ny, B, plane))
    left = lax.all_to_all(left, "y", split_axis=0, concat_axis=0, tiled=True)
    rights = [right] + [lax.ppermute(right, "z", [(a, (a + s) % nz) for a in range(nz)]) for s in range(1, nz)]

    partial = product(left, rights, z, ncore)
    partial = jnp.sum(lax.all_to_all(partial, "core", split_axis=0, concat_axis=0, tiled=True), axis=0)
    partial = jnp.sum(lax.all_to_all(partial, ("u", "v"), split_axis=0, concat_axis=0, tiled=True), axis=0)
    return partial.astype(jnp.bfloat16)


def solution(mesh):
    finer = Mesh(mesh.devices.reshape(8, 8, 2, 2, 2, 2), AXES)
    return jax.shard_map(
        body,
        mesh=finer,
        in_specs=(P(("z", "u", "v", "core"), None), P()),
        out_specs=P(("z", "u", "v", "core"), ("y", "w")),
        check_vma=False,
    )
```

```python
import jax
import jax.numpy as jnp
from jax import lax
from jax.experimental import pallas as pl
from jax.experimental.pallas import tpu as pltpu
from jax.sharding import Mesh, PartitionSpec as P

B = 128
AXES = ("z", "y", "w", "u", "v", "core")
TAIL = 16


def product_kernel(y_ref, *refs):
    *left_refs, right_ref, out_ref, ordered = refs
    n, depth, _ = right_ref.shape
    y = y_ref[0]

    @pl.when(pl.program_id(0) == 0)
    def _():
        for s in range(n):
            ordered[s * depth : (s + 1) * depth, :] = right_ref[lax.rem(y - s + n, n)]

    left = jnp.concatenate([r[...] for r in left_refs], axis=0)
    total = lax.dot_general(
        left, ordered[...], (((0,), (0,)), ((), ())), preferred_element_type=jnp.float32
    )
    cores, ways, rows, columns = out_ref.shape
    for a in range(cores):
        for b in range(ways):
            out_ref[a, b] = total[a * rows : (a + 1) * rows, b * columns : (b + 1) * columns]


def product(lefts, right, y, cores, ways):
    n, depth, wide = right.shape
    step = cores * B
    panel = wide // ways
    return pl.pallas_call(
        product_kernel,
        grid_spec=pltpu.PrefetchScalarGridSpec(
            num_scalar_prefetch=1,
            grid=(wide // step,),
            in_specs=[pl.BlockSpec((depth, step), lambda m, _: (0, m)) for _ in lefts]
            + [pl.BlockSpec((n, depth, wide), lambda m, _: (0, 0, 0))],
            out_specs=pl.BlockSpec((cores, ways, B, panel), lambda m, _: (0, m, 0, 0)),
            scratch_shapes=[pltpu.VMEM((n * depth, wide), right.dtype)],
        ),
        out_shape=jax.ShapeDtypeStruct((cores, wide // step * ways, B, panel), jnp.float32),
        compiler_params=pltpu.CompilerParams(vmem_limit_bytes=24 * 1024 * 1024),
        cost_estimate=pl.CostEstimate(
            flops=2 * n * depth * wide * wide,
            bytes_accessed=4 * n * depth * wide + 4 * wide * wide,
            transcendentals=0,
        ),
        name="product",
    )(y.reshape(1), *lefts, right)


def body(stored, pattern):
    nz, ny, nw, nu, nv, ncore = (lax.axis_size(a) for a in AXES)
    z, y, w, u, v, core = (lax.axis_index(a) for a in AXES)
    nl = nu * nv * ncore
    l = (u * nv + v) * ncore + core
    g = z * nl + l
    plane = nl * B
    part = B // nw

    raw = lax.dynamic_slice(stored, (0, y * plane), (B, plane))
    present = lax.dynamic_slice(pattern, (g, y * nl), (1, nl))
    present = jnp.repeat(present, B, axis=1) > 0
    row = g * B + jnp.arange(B, dtype=jnp.int32)[:, None]
    column = y * plane + jnp.arange(plane, dtype=jnp.int32)[None, :]
    band = jnp.where(present & (column >= row), raw, jnp.zeros((), raw.dtype))

    def flat(zz, yy, r):
        return (zz * ny + yy) * (nw * nl) + r

    mirror = [
        (flat(a, b, r), flat(b, a, r))
        for a in range(nz)
        for b in range(a + 1, ny)
        for r in range(nw * nl)
    ]

    turned = band.T.reshape(nl, nw, part, B)
    turned = lax.dynamic_index_in_dim(turned, w, 1, keepdims=False)
    crossed = lax.all_to_all(turned, ("u", "v", "core"), split_axis=0, concat_axis=0, tiled=True)
    straight = lax.dynamic_slice(band, (w * part, 0), (part, plane))
    straight_mirrored = lax.ppermute(straight, AXES, mirror)
    crossed, straight_mirrored = lax.optimization_barrier((crossed, straight_mirrored))
    crossed = crossed.transpose(1, 0, 2).reshape(part, plane)
    crossed_mirrored = lax.ppermute(crossed, AXES, mirror)
    straight = jnp.where(z <= y, straight, straight_mirrored)
    crossed = jnp.where(z <= y, crossed, crossed_mirrored)

    offset = l * B + w * part + jnp.arange(part, dtype=jnp.int32)[:, None]
    across = jnp.arange(plane, dtype=jnp.int32)[None, :]
    left = jnp.where(y * plane + offset <= z * plane + across, straight, crossed)
    right = jnp.where(z * plane + offset <= y * plane + across, straight, crossed)

    left, right = lax.optimization_barrier((left, right))
    right = jnp.broadcast_to(right[None], (nz, part, plane))
    right = lax.all_to_all(right, "z", split_axis=0, concat_axis=0, tiled=True)
    lefts = [left] + [lax.ppermute(left, "y", [(a, (a + s) % ny) for a in range(ny)]) for s in range(1, ny)]

    partial = product(lefts, right, y, ncore, nw)
    partial = jnp.sum(lax.all_to_all(partial, "core", split_axis=0, concat_axis=0, tiled=True), axis=0)

    most = jnp.max(jnp.abs(partial))
    power = jnp.clip(jnp.ceil(jnp.log2(jnp.maximum(most, 1e-30))) - 14.0, -100.0, 100.0)
    scaled = (partial * jnp.exp2(-power)).astype(jnp.float16)
    tail = jnp.broadcast_to(power.astype(jnp.float16), (scaled.shape[0], TAIL, scaled.shape[2]))
    sent = jnp.concatenate([scaled, tail], axis=1)
    got = lax.all_to_all(sent, ("u", "v", "w"), split_axis=0, concat_axis=0, tiled=True)
    scale = jnp.exp2(got[:, B, 0].astype(jnp.float32))
    total = jnp.sum(got[:, :B].astype(jnp.float32) * scale[:, None, None], axis=0)
    return total.astype(jnp.bfloat16)


def solution(mesh):
    finer = Mesh(mesh.devices.reshape(8, 8, 2, 2, 2, 2), AXES)
    return jax.shard_map(
        body,
        mesh=finer,
        in_specs=(P(("z", "u", "v", "core"), None), P()),
        out_specs=P(("z", "u", "v", "core"), ("y", "w")),
        check_vma=False,
    )
```

```python
import jax
import jax.numpy as jnp
from jax import lax
from jax.experimental import pallas as pl
from jax.experimental.pallas import tpu as pltpu
from jax.sharding import Mesh, PartitionSpec as P

B = 128
AXES = ("z", "y", "w", "u", "v", "core")
TAIL = 16


def product_kernel(z_ref, left_ref, right_ref, out_ref, ordered):
    n, depth, _ = right_ref.shape
    z = z_ref[0]

    @pl.when(pl.program_id(0) == 0)
    def _():
        for p in range(n):
            ordered[p * depth : (p + 1) * depth, :] = right_ref[lax.rem(p - z + n, n)]

    total = lax.dot_general(
        left_ref[...], ordered[...], (((0,), (0,)), ((), ())), preferred_element_type=jnp.float32
    )
    for a in range(out_ref.shape[0]):
        out_ref[a, 0] = total[a * B : (a + 1) * B]


def product(left, right, z, cores):
    n, depth, panel = right.shape
    wide = left.shape[1]
    step = cores * B
    return pl.pallas_call(
        product_kernel,
        grid_spec=pltpu.PrefetchScalarGridSpec(
            num_scalar_prefetch=1,
            grid=(wide // step,),
            in_specs=[
                pl.BlockSpec((n * depth, step), lambda m, _: (0, m)),
                pl.BlockSpec((n, depth, panel), lambda m, _: (0, 0, 0)),
            ],
            out_specs=pl.BlockSpec((cores, 1, B, panel), lambda m, _: (0, m, 0, 0)),
            scratch_shapes=[pltpu.VMEM((n * depth, panel), left.dtype)],
        ),
        out_shape=jax.ShapeDtypeStruct((cores, wide // step, B, panel), jnp.float32),
        compiler_params=pltpu.CompilerParams(vmem_limit_bytes=24 * 1024 * 1024),
        cost_estimate=pl.CostEstimate(
            flops=2 * n * depth * wide * panel,
            bytes_accessed=2 * n * depth * (wide + panel) + 4 * wide * panel,
            transcendentals=0,
        ),
        name="product",
    )(z.reshape(1), left, right)


def body(stored, pattern):
    nz, ny, nw, nu, nv, ncore = (lax.axis_size(a) for a in AXES)
    z, y, w, u, v, core = (lax.axis_index(a) for a in AXES)
    nl = nu * nv * ncore
    l = (u * nv + v) * ncore + core
    g = z * nl + l
    plane = nl * B
    panel = plane // nw

    def upper(first_block, blocks):
        raw = lax.dynamic_slice(stored, (0, first_block * B), (B, blocks * B))
        present = lax.dynamic_slice(pattern, (g, first_block), (1, blocks))
        present = jnp.repeat(present, B, axis=1) > 0
        row = g * B + jnp.arange(B, dtype=jnp.int32)[:, None]
        column = first_block * B + jnp.arange(blocks * B, dtype=jnp.int32)[None, :]
        return jnp.where(present & (column >= row), raw, jnp.zeros((), raw.dtype))

    def flat(zz, yy, r):
        return (zz * ny + yy) * (nw * nl) + r

    def pairs(target, least):
        found = []
        for a in range(nz):
            for b in range(ny):
                c = (b - a) % nz
                if c >= a + least:
                    found += [(flat(a, b, r), flat(*target(a, b, c), r)) for r in range(nw * nl)]
        return found

    k = lax.rem(y - z + nz, nz)
    band = upper(k * nl, nl)
    turned = band.T.reshape(nl, B, B)
    crossed = lax.all_to_all(turned, ("u", "v", "core"), split_axis=0, concat_axis=0, tiled=True)
    straight = lax.ppermute(band, AXES, pairs(lambda a, b, c: (c, b), 1))
    crossed = crossed.transpose(1, 0, 2).reshape(B, plane)
    offset = l * B + jnp.arange(B, dtype=jnp.int32)[:, None]
    across = jnp.arange(plane, dtype=jnp.int32)[None, :]
    left = jnp.where(
        k * plane + offset <= z * plane + across, jnp.where(k == z, band, straight), crossed
    )
    left = lax.all_gather(left, "y", axis=0, tiled=True)

    half = lax.dynamic_slice(crossed, (0, w * panel), (B, panel))
    half = lax.ppermute(half, AXES, pairs(lambda a, b, c: (c, a), 0))
    tile = upper(y * nl + w * (nl // nw), nl // nw)
    own = y * plane + w * panel + jnp.arange(panel, dtype=jnp.int32)[None, :]
    right = jnp.where(z * plane + offset <= own, tile, half)
    right = jnp.broadcast_to(right[None], (nz, B, panel))
    right = lax.all_to_all(right, "z", split_axis=0, concat_axis=0, tiled=True)

    partial = product(left, right, z, ncore)
    partial = jnp.sum(lax.all_to_all(partial, "core", split_axis=0, concat_axis=0, tiled=True), axis=0)

    most = jnp.max(jnp.abs(partial))
    power = jnp.clip(jnp.ceil(jnp.log2(jnp.maximum(most, 1e-30))) - 14.0, -100.0, 100.0)
    grown = jnp.exp2(-power)
    tail = jnp.broadcast_to(power.astype(jnp.float16), (TAIL, panel))
    mine = u * nv + v
    total = lax.dynamic_index_in_dim(partial, mine, 0, keepdims=False)
    for d in range(1, nu * nv):
        chunk = lax.dynamic_index_in_dim(partial, mine ^ d, 0, keepdims=False)
        chunk = jnp.concatenate([(chunk * grown).astype(jnp.float16), tail], axis=0)
        got = lax.ppermute(chunk, ("u", "v"), [(a, a ^ d) for a in range(nu * nv)])
        total = total + got[:B].astype(jnp.float32) * jnp.exp2(got[B:, :1].astype(jnp.float32)[:1])
    return total.astype(jnp.bfloat16)


def solution(mesh):
    finer = Mesh(mesh.devices.reshape(8, 8, 2, 2, 2, 2), AXES)
    return jax.shard_map(
        body,
        mesh=finer,
        in_specs=(P(("z", "u", "v", "core"), None), P()),
        out_specs=P(("z", "u", "v", "core"), ("y", "w")),
        check_vma=False,
    )
```

```python
import jax
import jax.numpy as jnp
from jax import lax
from jax.experimental import pallas as pl
from jax.experimental.pallas import tpu as pltpu
from jax.sharding import Mesh, PartitionSpec as P

B = 128
AXES = ("z", "y", "w", "u", "v", "core")
TAIL = 16


def product_kernel(z_ref, left_ref, right_ref, out_ref, ordered):
    n, depth, _ = right_ref.shape
    z = z_ref[0]

    @pl.when(pl.program_id(0) == 0)
    def _():
        for p in range(n):
            ordered[p * depth : (p + 1) * depth, :] = right_ref[lax.rem(p - z + n, n)]

    total = lax.dot_general(
        left_ref[...], ordered[...], (((0,), (0,)), ((), ())), preferred_element_type=jnp.float32
    )
    for a in range(out_ref.shape[0]):
        out_ref[a, 0] = total[a * B : (a + 1) * B]


def product(left, right, z, cores):
    n, depth, panel = right.shape
    wide = left.shape[1]
    step = cores * B
    return pl.pallas_call(
        product_kernel,
        grid_spec=pltpu.PrefetchScalarGridSpec(
            num_scalar_prefetch=1,
            grid=(wide // step,),
            in_specs=[
                pl.BlockSpec((n * depth, step), lambda m, _: (0, m)),
                pl.BlockSpec((n, depth, panel), lambda m, _: (0, 0, 0)),
            ],
            out_specs=pl.BlockSpec((cores, 1, B, panel), lambda m, _: (0, m, 0, 0)),
            scratch_shapes=[pltpu.VMEM((n * depth, panel), left.dtype)],
        ),
        out_shape=jax.ShapeDtypeStruct((cores, wide // step, B, panel), jnp.float32),
        compiler_params=pltpu.CompilerParams(vmem_limit_bytes=24 * 1024 * 1024),
        cost_estimate=pl.CostEstimate(
            flops=2 * n * depth * wide * panel,
            bytes_accessed=2 * n * depth * (wide + panel) + 4 * wide * panel,
            transcendentals=0,
        ),
        name="product",
    )(z.reshape(1), left, right)


def body(stored, pattern):
    nz, ny, nw, nu, nv, ncore = (lax.axis_size(a) for a in AXES)
    z, y, w, u, v, core = (lax.axis_index(a) for a in AXES)
    nl = nu * nv * ncore
    l = (u * nv + v) * ncore + core
    g = z * nl + l
    plane = nl * B
    panel = plane // nw

    def columns(start, width):
        return lax.dynamic_slice(stored, (0, start), (B, width))

    def here(rows, first, count, across):
        if across:
            found = lax.dynamic_slice(pattern, (rows, first), (1, count))
        else:
            found = lax.dynamic_slice(pattern, (first, rows), (count, 1)).reshape(1, count)
        return jnp.repeat(found, B, axis=1) > 0

    def flat(zz, yy, r):
        return (zz * ny + yy) * (nw * nl) + r

    def pairs(target, least):
        found = []
        for a in range(nz):
            for b in range(ny):
                c = (b - a) % nz
                if c >= a + least:
                    found += [(flat(a, b, r), flat(*target(a, b, c), r)) for r in range(nw * nl)]
        return found

    k = lax.rem(y - z + nz, nz)
    band = columns(k * plane, plane)
    straight = lax.ppermute(band, AXES, pairs(lambda a, b, c: (c, b), 1))
    turned = band.T.reshape(nl, B, B)
    crossed = lax.all_to_all(turned, ("u", "v", "core"), split_axis=0, concat_axis=0, tiled=True)
    first = y * nl + w * (nl // nw)
    present = (
        here(k * nl + l, z * nl, nl, True),
        here(k * nl + l, z * nl, nl, False),
        here(g, first, nl // nw, True),
        here(g, first, nl // nw, False),
    )
    crossed, present = lax.optimization_barrier((crossed, present))
    crossed = crossed.transpose(1, 0, 2).reshape(B, plane)
    zero = jnp.zeros((), stored.dtype)
    offset = l * B + jnp.arange(B, dtype=jnp.int32)[:, None]
    across = jnp.arange(plane, dtype=jnp.int32)[None, :]
    above = k * plane + offset <= z * plane + across
    kept = jnp.where(above, present[0], present[1])
    left = jnp.where(kept, jnp.where(above, jnp.where(k == z, band, straight), crossed), zero)
    left = lax.all_gather(left, "y", axis=0, tiled=True)

    half = lax.dynamic_slice(crossed, (0, w * panel), (B, panel))
    half = lax.ppermute(half, AXES, pairs(lambda a, b, c: (c, a), 0))
    tile = columns(y * plane + w * panel, panel)
    own = y * plane + w * panel + jnp.arange(panel, dtype=jnp.int32)[None, :]
    above = z * plane + offset <= own
    kept = jnp.where(above, present[2], present[3])
    right = jnp.where(kept, jnp.where(above, tile, half), zero)
    right = jnp.broadcast_to(right[None], (nz, B, panel))
    right = lax.all_to_all(right, "z", split_axis=0, concat_axis=0, tiled=True)

    partial = product(left, right, z, ncore)
    partial = jnp.sum(lax.all_to_all(partial, "core", split_axis=0, concat_axis=0, tiled=True), axis=0)

    most = jnp.max(jnp.abs(partial))
    power = jnp.clip(jnp.ceil(jnp.log2(jnp.maximum(most, 1e-30))) - 14.0, -100.0, 100.0)
    grown = jnp.exp2(-power)
    tail = jnp.broadcast_to(power.astype(jnp.float16), (TAIL, panel))
    mine = u * nv + v
    total = 0.0
    for d in range(1, nu * nv):
        chunk = lax.dynamic_index_in_dim(partial, mine ^ d, 0, keepdims=False)
        chunk = jnp.concatenate([(chunk * grown).astype(jnp.float16), tail], axis=0)
        got = lax.ppermute(chunk, ("u", "v"), [(a, a ^ d) for a in range(nu * nv)])
        total = total + got.astype(jnp.float32) * jnp.exp2(got[B, 0].astype(jnp.float32))
    total = total[:B] + lax.dynamic_index_in_dim(partial, mine, 0, keepdims=False)
    return total.astype(jnp.bfloat16)


def solution(mesh):
    finer = Mesh(mesh.devices.reshape(8, 8, 2, 2, 2, 2), AXES)
    return jax.shard_map(
        body,
        mesh=finer,
        in_specs=(P(("z", "u", "v", "core"), None), P()),
        out_specs=P(("z", "u", "v", "core"), ("y", "w")),
        check_vma=False,
    )
```

```python
import jax
import jax.numpy as jnp
from jax import lax
from jax.experimental import pallas as pl
from jax.experimental.pallas import tpu as pltpu
from jax.sharding import Mesh, PartitionSpec as P

B = 128
AXES = ("z", "y", "w", "u", "v", "core")
TAIL = 16


def blocks_kernel(k_ref, stored_ref, band_ref, turned_ref):
    band_ref[...] = stored_ref[...]
    for j in range(turned_ref.shape[0]):
        turned_ref[j] = stored_ref[:, j * B : (j + 1) * B].T


def blocks(stored, k, wide):
    count = wide // B
    return pl.pallas_call(
        blocks_kernel,
        grid_spec=pltpu.PrefetchScalarGridSpec(
            num_scalar_prefetch=1,
            grid=(1,),
            in_specs=[pl.BlockSpec((B, wide), lambda m, k_ref: (0, k_ref[0]))],
            out_specs=[
                pl.BlockSpec((B, wide), lambda m, _: (0, 0)),
                pl.BlockSpec((count, B, B), lambda m, _: (0, 0, 0)),
            ],
        ),
        out_shape=[
            jax.ShapeDtypeStruct((B, wide), stored.dtype),
            jax.ShapeDtypeStruct((count, B, B), stored.dtype),
        ],
        cost_estimate=pl.CostEstimate(flops=0, bytes_accessed=6 * B * wide, transcendentals=0),
        name="blocks",
    )(k.reshape(1), stored)


def left_kernel(at_ref, band_ref, straight_ref, crossed_ref, row_ref, column_ref, out_ref):
    k, z, l = at_ref[0], at_ref[1], at_ref[2]
    count = crossed_ref.shape[0]
    position = k * count * B + l * B + lax.broadcasted_iota(jnp.int32, (B, B), 0)
    for j in range(count):
        part = slice(j * B, (j + 1) * B)
        across = (z * count + j) * B + lax.broadcasted_iota(jnp.int32, (B, B), 1)
        band = band_ref[:, part].astype(jnp.float32)
        straight = jnp.where(k == z, band, straight_ref[:, part].astype(jnp.float32))
        straight = straight * row_ref[:, part]
        crossed = crossed_ref[j].astype(jnp.float32) * column_ref[:, part]
        out_ref[:, part] = jnp.where(position <= across, straight, crossed).astype(out_ref.dtype)


def left_piece(at, band, straight, crossed, row, column):
    rows, wide = band.shape
    whole = pl.BlockSpec((rows, wide), lambda m, _: (0, 0))
    vector = pl.BlockSpec((1, wide), lambda m, _: (0, 0))
    return pl.pallas_call(
        left_kernel,
        grid_spec=pltpu.PrefetchScalarGridSpec(
            num_scalar_prefetch=1,
            grid=(1,),
            in_specs=[whole, whole, pl.BlockSpec(crossed.shape, lambda m, _: (0, 0, 0)), vector, vector],
            out_specs=whole,
        ),
        out_shape=jax.ShapeDtypeStruct((rows, wide), band.dtype),
        cost_estimate=pl.CostEstimate(flops=0, bytes_accessed=8 * rows * wide, transcendentals=0),
        name="left_piece",
    )(at, band, straight, crossed, row, column)


def product_kernel(z_ref, left_ref, right_ref, out_ref, ordered, buffer, arrived):
    n, depth, _ = right_ref.shape
    count, _, step = buffer.shape
    z = z_ref[0]
    copies = [
        pltpu.make_async_copy(left_ref.at[:, m * step : (m + 1) * step], buffer.at[m], arrived.at[m])
        for m in range(count)
    ]
    for copy in copies:
        copy.start()
    for p in range(n):
        ordered[p * depth : (p + 1) * depth, :] = right_ref[lax.rem(p - z + n, n)]
    for m, copy in enumerate(copies):
        copy.wait()
        total = lax.dot_general(
            buffer[m], ordered[...], (((0,), (0,)), ((), ())), preferred_element_type=jnp.float32
        )
        for a in range(out_ref.shape[0]):
            out_ref[a, m] = total[a * B : (a + 1) * B]


def product(left, right, z, cores):
    n, depth, panel = right.shape
    wide = left.shape[1]
    step = cores * B
    return pl.pallas_call(
        product_kernel,
        in_specs=[
            pl.BlockSpec(memory_space=pltpu.SMEM),
            pl.BlockSpec(memory_space=pltpu.HBM),
            pl.BlockSpec(memory_space=pltpu.VMEM),
        ],
        out_specs=pl.BlockSpec(memory_space=pltpu.VMEM),
        scratch_shapes=[
            pltpu.VMEM((n * depth, panel), left.dtype),
            pltpu.VMEM((wide // step, n * depth, step), left.dtype),
            pltpu.SemaphoreType.DMA((wide // step,)),
        ],
        out_shape=jax.ShapeDtypeStruct((cores, wide // step, B, panel), jnp.float32),
        compiler_params=pltpu.CompilerParams(vmem_limit_bytes=24 * 1024 * 1024),
        cost_estimate=pl.CostEstimate(
            flops=2 * n * depth * wide * panel,
            bytes_accessed=2 * n * depth * (wide + panel) + 4 * wide * panel,
            transcendentals=0,
        ),
        name="product",
    )(z.reshape(1), left, right)


def body(stored, pattern):
    nz, ny, nw, nu, nv, ncore = (lax.axis_size(a) for a in AXES)
    z, y, w, u, v, core = (lax.axis_index(a) for a in AXES)
    nl = nu * nv * ncore
    l = (u * nv + v) * ncore + core
    g = z * nl + l
    plane = nl * B
    panel = plane // nw

    def columns(start, width):
        return lax.dynamic_slice(stored, (0, start), (B, width))

    def here(rows, first, count, across):
        if across:
            found = lax.dynamic_slice(pattern, (rows, first), (1, count))
        else:
            found = lax.dynamic_slice(pattern, (first, rows), (count, 1)).reshape(1, count)
        return jnp.repeat(found, B, axis=1) > 0

    def flat(zz, yy, r):
        return (zz * ny + yy) * (nw * nl) + r

    def pairs(target, least):
        found = []
        for a in range(nz):
            for b in range(ny):
                c = (b - a) % nz
                if c >= a + least:
                    found += [(flat(a, b, r), flat(*target(a, b, c), r)) for r in range(nw * nl)]
        return found

    k = lax.rem(y - z + nz, nz)
    band, turned = blocks(stored, k, plane)
    straight = lax.ppermute(band, AXES, pairs(lambda a, b, c: (c, b), 1))
    crossed = lax.all_to_all(turned, ("u", "v", "core"), split_axis=0, concat_axis=0, tiled=True)
    first = y * nl + w * (nl // nw)
    present = (
        here(k * nl + l, z * nl, nl, True).astype(jnp.float32),
        here(k * nl + l, z * nl, nl, False).astype(jnp.float32),
        here(g, first, nl // nw, True),
        here(g, first, nl // nw, False),
    )
    crossed, present = lax.optimization_barrier((crossed, present))
    left = left_piece(
        jnp.stack([k, z, l]),
        band,
        straight,
        crossed,
        present[0],
        present[1],
    )
    left = lax.all_gather(left, "y", axis=0, tiled=True)

    half = lax.dynamic_slice(crossed, (w * (nl // nw), 0, 0), (nl // nw, B, B))
    half = half.transpose(1, 0, 2).reshape(B, panel)
    half = lax.ppermute(half, AXES, pairs(lambda a, b, c: (c, a), 0))
    tile = columns(y * plane + w * panel, panel)
    own = y * plane + w * panel + jnp.arange(panel, dtype=jnp.int32)[None, :]
    offset = l * B + jnp.arange(B, dtype=jnp.int32)[:, None]
    above = z * plane + offset <= own
    kept = jnp.where(above, present[2], present[3])
    right = jnp.where(kept, jnp.where(above, tile, half), jnp.zeros((), stored.dtype))
    right = jnp.broadcast_to(right[None], (nz, B, panel))
    right = lax.all_to_all(right, "z", split_axis=0, concat_axis=0, tiled=True)

    partial = product(left, right, z, ncore)
    partial = jnp.sum(lax.all_to_all(partial, "core", split_axis=0, concat_axis=0, tiled=True), axis=0)

    most = jnp.max(jnp.abs(partial))
    power = jnp.clip(jnp.ceil(jnp.log2(jnp.maximum(most, 1e-30))) - 14.0, -100.0, 100.0)
    grown = jnp.exp2(-power)
    tail = jnp.broadcast_to(power.astype(jnp.float16), (TAIL, panel))
    mine = u * nv + v
    total = 0.0
    for d in range(1, nu * nv):
        chunk = lax.dynamic_index_in_dim(partial, mine ^ d, 0, keepdims=False)
        chunk = jnp.concatenate([(chunk * grown).astype(jnp.float16), tail], axis=0)
        got = lax.ppermute(chunk, ("u", "v"), [(a, a ^ d) for a in range(nu * nv)])
        total = total + got.astype(jnp.float32) * jnp.exp2(got[B, 0].astype(jnp.float32))
    total = total[:B] + lax.dynamic_index_in_dim(partial, mine, 0, keepdims=False)
    return total.astype(jnp.bfloat16)


def solution(mesh):
    finer = Mesh(mesh.devices.reshape(8, 8, 2, 2, 2, 2), AXES)
    return jax.shard_map(
        body,
        mesh=finer,
        in_specs=(P(("z", "u", "v", "core"), None), P()),
        out_specs=P(("z", "u", "v", "core"), ("y", "w")),
        check_vma=False,
    )
```

```python
import jax
import jax.numpy as jnp
from jax import lax
from jax.experimental import pallas as pl
from jax.experimental.pallas import tpu as pltpu
from jax.experimental.layout import Layout, with_layout_constraint
from jax.sharding import Mesh, PartitionSpec as P

B = 128
AXES = ("z", "y", "w", "u", "v", "core")
TAIL = 16


def product_kernel(z_ref, left_ref, right_ref, out_ref, ordered):
    n, depth, _ = right_ref.shape
    z = z_ref[0]

    @pl.when(pl.program_id(0) == 0)
    def _():
        for p in range(n):
            ordered[p * depth : (p + 1) * depth, :] = right_ref[lax.rem(p - z + n, n)]

    for a in range(out_ref.shape[0]):
        out_ref[a, 0] = lax.dot_general(
            left_ref[:, a].reshape(n * depth, B),
            ordered[...],
            (((0,), (0,)), ((), ())),
            preferred_element_type=jnp.float32,
        )


def product(left, right, z, cores):
    n, depth, panel = right.shape
    wide = left.shape[1] * B
    step = cores * B
    return pl.pallas_call(
        product_kernel,
        grid_spec=pltpu.PrefetchScalarGridSpec(
            num_scalar_prefetch=1,
            grid=(wide // step,),
            in_specs=[
                pl.BlockSpec((n, cores, depth, B), lambda m, _: (0, m, 0, 0)),
                pl.BlockSpec((n, depth, panel), lambda m, _: (0, 0, 0)),
            ],
            out_specs=pl.BlockSpec((cores, 1, B, panel), lambda m, _: (0, m, 0, 0)),
            scratch_shapes=[pltpu.VMEM((n * depth, panel), left.dtype)],
        ),
        out_shape=jax.ShapeDtypeStruct((cores, wide // step, B, panel), jnp.float32),
        compiler_params=pltpu.CompilerParams(vmem_limit_bytes=56 * 1024 * 1024),
        cost_estimate=pl.CostEstimate(
            flops=2 * n * depth * wide * panel,
            bytes_accessed=2 * n * depth * (wide + panel) + 4 * wide * panel,
            transcendentals=0,
        ),
        name="product",
    )(z.reshape(1), left, right)


def body(stored, pattern):
    nz, ny, nw, nu, nv, ncore = (lax.axis_size(a) for a in AXES)
    z, y, w, u, v, core = (lax.axis_index(a) for a in AXES)
    nl = nu * nv * ncore
    l = (u * nv + v) * ncore + core
    g = z * nl + l
    plane = nl * B
    panel = plane // nw

    def columns(start, width):
        return lax.dynamic_slice(stored, (0, start), (B, width))

    def here(rows, first, count, across):
        if across:
            found = lax.dynamic_slice(pattern, (rows, first), (1, count))
        else:
            found = lax.dynamic_slice(pattern, (first, rows), (count, 1)).reshape(1, count)
        return jnp.repeat(found, B, axis=1) > 0

    def flat(zz, yy, r):
        return (zz * ny + yy) * (nw * nl) + r

    def pairs(target, least):
        found = []
        for a in range(nz):
            for b in range(ny):
                c = (b - a) % nz
                if c >= a + least:
                    found += [(flat(a, b, r), flat(*target(a, b, c), r)) for r in range(nw * nl)]
        return found

    k = lax.rem(y - z + nz, nz)
    band = columns(k * plane, plane).reshape(B, nl, B).transpose(1, 0, 2)
    straight = lax.ppermute(band, AXES, pairs(lambda a, b, c: (c, b), 1))
    turned = columns(k * plane, plane).T.reshape(nl, B, B)
    crossed = lax.all_to_all(turned, ("u", "v", "core"), split_axis=0, concat_axis=0, tiled=True)
    first = y * nl + w * (nl // nw)
    present = (
        here(k * nl + l, z * nl, nl, True),
        here(k * nl + l, z * nl, nl, False),
        here(g, first, nl // nw, True),
        here(g, first, nl // nw, False),
    )
    crossed, present = lax.optimization_barrier((crossed, present))
    zero = jnp.zeros((), stored.dtype)
    offset = l * B + jnp.arange(B, dtype=jnp.int32)
    across = jnp.arange(plane, dtype=jnp.int32).reshape(nl, 1, B)
    above = k * plane + offset[None, :, None] <= z * plane + across
    kept = jnp.where(above, present[0].reshape(nl, 1, B), present[1].reshape(nl, 1, B))
    left = jnp.where(kept, jnp.where(above, jnp.where(k == z, band, straight), crossed), zero)
    left = lax.all_gather(left, "y", axis=0, tiled=True).reshape(ny, nl, B, B)

    half = with_layout_constraint(crossed.transpose(1, 0, 2).reshape(B, plane), Layout((0, 1)))
    half = lax.dynamic_slice(half, (0, w * panel), (B, panel))
    half = lax.ppermute(half, AXES, pairs(lambda a, b, c: (c, a), 0))
    tile = columns(y * plane + w * panel, panel)
    own = y * plane + w * panel + jnp.arange(panel, dtype=jnp.int32)[None, :]
    above = z * plane + offset[:, None] <= own
    kept = jnp.where(above, present[2], present[3])
    right = jnp.where(kept, jnp.where(above, tile, half), zero)
    right = jnp.broadcast_to(right[None], (nz, B, panel))
    right = lax.all_to_all(right, "z", split_axis=0, concat_axis=0, tiled=True)

    partial = product(left, right, z, ncore)
    partial = jnp.sum(lax.all_to_all(partial, "core", split_axis=0, concat_axis=0, tiled=True), axis=0)

    most = jnp.max(jnp.abs(partial))
    power = jnp.clip(jnp.ceil(jnp.log2(jnp.maximum(most, 1e-30))) - 14.0, -100.0, 100.0)
    grown = jnp.exp2(-power)
    tail = jnp.broadcast_to(power.astype(jnp.float16), (TAIL, panel))
    mine = u * nv + v
    total = 0.0
    for d in range(1, nu * nv):
        chunk = lax.dynamic_index_in_dim(partial, mine ^ d, 0, keepdims=False)
        chunk = jnp.concatenate([(chunk * grown).astype(jnp.float16), tail], axis=0)
        got = lax.ppermute(chunk, ("u", "v"), [(a, a ^ d) for a in range(nu * nv)])
        total = total + got.astype(jnp.float32) * jnp.exp2(got[B, 0].astype(jnp.float32))
    total = total[:B] + lax.dynamic_index_in_dim(partial, mine, 0, keepdims=False)
    return total.astype(jnp.bfloat16)


def solution(mesh):
    finer = Mesh(mesh.devices.reshape(8, 8, 2, 2, 2, 2), AXES)
    return jax.shard_map(
        body,
        mesh=finer,
        in_specs=(P(("z", "u", "v", "core"), None), P()),
        out_specs=P(("z", "u", "v", "core"), ("y", "w")),
        check_vma=False,
    )
```

```python
import jax
import jax.numpy as jnp
from jax import lax
from jax.experimental import pallas as pl
from jax.experimental.pallas import tpu as pltpu
from jax.experimental.layout import Layout, with_layout_constraint
from jax.sharding import Mesh, PartitionSpec as P

B = 128
AXES = ("z", "y", "w", "u", "v", "core")
TAIL = 16


def product_kernel(z_ref, left_ref, right_ref, out_ref, ordered):
    n, depth, _ = right_ref.shape
    z = z_ref[0]

    @pl.when(pl.program_id(0) == 0)
    def _():
        for p in range(n):
            ordered[p * depth : (p + 1) * depth, :] = right_ref[lax.rem(p - z + n, n)]

    for a in range(out_ref.shape[0]):
        out_ref[a, 0] = lax.dot_general(
            left_ref[:, a].reshape(n * depth, B),
            ordered[...],
            (((0,), (0,)), ((), ())),
            preferred_element_type=jnp.float32,
        )


def product(left, right, z, cores):
    n, depth, panel = right.shape
    wide = left.shape[1] * B
    step = cores * B
    return pl.pallas_call(
        product_kernel,
        grid_spec=pltpu.PrefetchScalarGridSpec(
            num_scalar_prefetch=1,
            grid=(wide // step,),
            in_specs=[
                pl.BlockSpec((n, cores, depth, B), lambda m, _: (0, m, 0, 0)),
                pl.BlockSpec((n, depth, panel), lambda m, _: (0, 0, 0)),
            ],
            out_specs=pl.BlockSpec((cores, 1, B, panel), lambda m, _: (0, m, 0, 0)),
            scratch_shapes=[pltpu.VMEM((n * depth, panel), left.dtype)],
        ),
        out_shape=jax.ShapeDtypeStruct((cores, wide // step, B, panel), jnp.float32),
        compiler_params=pltpu.CompilerParams(vmem_limit_bytes=24 * 1024 * 1024),
        cost_estimate=pl.CostEstimate(
            flops=2 * n * depth * wide * panel,
            bytes_accessed=2 * n * depth * (wide + panel) + 4 * wide * panel,
            transcendentals=0,
        ),
        name="product",
    )(z.reshape(1), left, right)


def body(stored, pattern):
    nz, ny, nw, nu, nv, ncore = (lax.axis_size(a) for a in AXES)
    z, y, w, u, v, core = (lax.axis_index(a) for a in AXES)
    nl = nu * nv * ncore
    l = (u * nv + v) * ncore + core
    g = z * nl + l
    plane = nl * B
    panel = plane // nw

    def columns(start, width):
        return lax.dynamic_slice(stored, (0, start), (B, width))

    def here(rows, first, count, across):
        if across:
            found = lax.dynamic_slice(pattern, (rows, first), (1, count))
        else:
            found = lax.dynamic_slice(pattern, (first, rows), (count, 1)).reshape(1, count)
        return jnp.repeat(found, B, axis=1) > 0

    def flat(zz, yy, r):
        return (zz * ny + yy) * (nw * nl) + r

    def pairs(target, least):
        found = []
        for a in range(nz):
            for b in range(ny):
                c = (b - a) % nz
                if c >= a + least:
                    found += [(flat(a, b, r), flat(*target(a, b, c), r)) for r in range(nw * nl)]
        return found

    k = lax.rem(y - z + nz, nz)
    band = columns(k * plane, plane).reshape(B, nl, B).transpose(1, 0, 2)
    straight = lax.ppermute(band, AXES, pairs(lambda a, b, c: (c, b), 1))
    turned = columns(k * plane, plane).T.reshape(nl, B, B)
    crossed = lax.all_to_all(turned, ("u", "v", "core"), split_axis=0, concat_axis=0, tiled=True)
    first = y * nl + w * (nl // nw)
    present = (
        here(k * nl + l, z * nl, nl, True),
        here(k * nl + l, z * nl, nl, False),
        here(g, first, nl // nw, True),
        here(g, first, nl // nw, False),
    )
    crossed, present = lax.optimization_barrier((crossed, present))
    zero = jnp.zeros((), stored.dtype)
    offset = l * B + jnp.arange(B, dtype=jnp.int32)
    across = jnp.arange(plane, dtype=jnp.int32).reshape(nl, 1, B)
    above = k * plane + offset[None, :, None] <= z * plane + across
    kept = jnp.where(above, present[0].reshape(nl, 1, B), present[1].reshape(nl, 1, B))
    left = jnp.where(kept, jnp.where(above, jnp.where(k == z, band, straight), crossed), zero)
    left = lax.all_gather(left, "y", axis=0, tiled=True).reshape(ny, nl, B, B)

    half = with_layout_constraint(crossed.transpose(1, 0, 2).reshape(B, plane), Layout((0, 1)))
    half = lax.dynamic_slice(half, (0, w * panel), (B, panel))
    half = lax.ppermute(half, AXES, pairs(lambda a, b, c: (c, a), 0))
    tile = columns(y * plane + w * panel, panel)
    own = y * plane + w * panel + jnp.arange(panel, dtype=jnp.int32)[None, :]
    above = z * plane + offset[:, None] <= own
    kept = jnp.where(above, present[2], present[3])
    right = jnp.where(kept, jnp.where(above, tile, half), zero)
    right = jnp.broadcast_to(right[None], (nz, B, panel))
    right = lax.all_to_all(right, "z", split_axis=0, concat_axis=0, tiled=True)

    partial = product(left, right, z, ncore)
    partial = jnp.sum(lax.all_to_all(partial, "core", split_axis=0, concat_axis=0, tiled=True), axis=0)

    most = jnp.max(jnp.abs(partial))
    power = jnp.clip(jnp.ceil(jnp.log2(jnp.maximum(most, 1e-30))) - 14.0, -100.0, 100.0)
    grown = jnp.exp2(-power)
    tail = jnp.broadcast_to(power.astype(jnp.float16), (TAIL, panel))
    mine = u * nv + v
    total = 0.0
    for d in range(1, nu * nv):
        chunk = lax.dynamic_index_in_dim(partial, mine ^ d, 0, keepdims=False)
        chunk = jnp.concatenate([(chunk * grown).astype(jnp.float16), tail], axis=0)
        got = lax.ppermute(chunk, ("u", "v"), [(a, a ^ d) for a in range(nu * nv)])
        total = total + got.astype(jnp.float32) * jnp.exp2(got[B : B + 1].astype(jnp.float32))
    total = total[:B] + lax.dynamic_index_in_dim(partial, mine, 0, keepdims=False)
    return total.astype(jnp.bfloat16)


def solution(mesh):
    finer = Mesh(mesh.devices.reshape(8, 8, 2, 2, 2, 2), AXES)
    return jax.shard_map(
        body,
        mesh=finer,
        in_specs=(P(("z", "u", "v", "core"), None), P()),
        out_specs=P(("z", "u", "v", "core"), ("y", "w")),
        check_vma=False,
    )
```

```python
import jax
import jax.numpy as jnp
from jax import lax
from jax.experimental import pallas as pl
from jax.experimental.pallas import tpu as pltpu
from jax.experimental.layout import Layout, with_layout_constraint
from jax.sharding import Mesh, PartitionSpec as P

B = 128
AXES = ("z", "y", "w", "u", "v", "core")
TAIL = 16


def product_kernel(z_ref, left_ref, right_ref, out_ref, ordered):
    n, depth, _ = right_ref.shape
    z = z_ref[0]

    @pl.when(pl.program_id(0) == 0)
    def _():
        for p in range(n):
            ordered[p * depth : (p + 1) * depth, :] = right_ref[lax.rem(p - z + n, n)]

    for a in range(out_ref.shape[0]):
        out_ref[a, 0] = lax.dot_general(
            left_ref[:, a].reshape(n * depth, B),
            ordered[...],
            (((0,), (0,)), ((), ())),
            preferred_element_type=jnp.float32,
        )


def product(left, right, z, cores):
    n, depth, panel = right.shape
    wide = left.shape[1] * B
    step = cores * B
    return pl.pallas_call(
        product_kernel,
        grid_spec=pltpu.PrefetchScalarGridSpec(
            num_scalar_prefetch=1,
            grid=(wide // step,),
            in_specs=[
                pl.BlockSpec((n, cores, depth, B), lambda m, _: (0, m, 0, 0)),
                pl.BlockSpec((n, depth, panel), lambda m, _: (0, 0, 0)),
            ],
            out_specs=pl.BlockSpec((cores, 1, B, panel), lambda m, _: (0, m, 0, 0)),
            scratch_shapes=[pltpu.VMEM((n * depth, panel), left.dtype)],
        ),
        out_shape=jax.ShapeDtypeStruct((cores, wide // step, B, panel), jnp.float32),
        compiler_params=pltpu.CompilerParams(vmem_limit_bytes=50 * 1024 * 1024),
        cost_estimate=pl.CostEstimate(
            flops=2 * n * depth * wide * panel,
            bytes_accessed=2 * n * depth * (wide + panel) + 4 * wide * panel,
            transcendentals=0,
        ),
        name="product",
    )(z.reshape(1), left, right)


def body(stored, pattern):
    nz, ny, nw, nu, nv, ncore = (lax.axis_size(a) for a in AXES)
    z, y, w, u, v, core = (lax.axis_index(a) for a in AXES)
    nl = nu * nv * ncore
    l = (u * nv + v) * ncore + core
    g = z * nl + l
    plane = nl * B
    panel = plane // nw

    def columns(start, width):
        return lax.dynamic_slice(stored, (0, start), (B, width))

    def here(rows, first, count, across):
        if across:
            found = lax.dynamic_slice(pattern, (rows, first), (1, count))
        else:
            found = lax.dynamic_slice(pattern, (first, rows), (count, 1)).reshape(1, count)
        return jnp.repeat(found, B, axis=1) > 0

    def flat(zz, yy, r):
        return (zz * ny + yy) * (nw * nl) + r

    def pairs(target, least):
        found = []
        for a in range(nz):
            for b in range(ny):
                c = (b - a) % nz
                if c >= a + least:
                    found += [(flat(a, b, r), flat(*target(a, b, c), r)) for r in range(nw * nl)]
        return found

    k = lax.rem(y - z + nz, nz)
    band = columns(k * plane, plane).reshape(B, nl, B).transpose(1, 0, 2)
    straight = lax.ppermute(band, AXES, pairs(lambda a, b, c: (c, b), 1))
    turned = columns(k * plane, plane).T.reshape(nl, B, B)
    crossed = lax.all_to_all(turned, ("u", "v", "core"), split_axis=0, concat_axis=0, tiled=True)
    first = y * nl + w * (nl // nw)
    present = (
        here(k * nl + l, z * nl, nl, True),
        here(k * nl + l, z * nl, nl, False),
        here(g, first, nl // nw, True),
        here(g, first, nl // nw, False),
    )
    crossed, present = lax.optimization_barrier((crossed, present))
    zero = jnp.zeros((), stored.dtype)
    offset = l * B + jnp.arange(B, dtype=jnp.int32)
    across = jnp.arange(plane, dtype=jnp.int32).reshape(nl, 1, B)
    above = k * plane + offset[None, :, None] <= z * plane + across
    kept = jnp.where(above, present[0].reshape(nl, 1, B), present[1].reshape(nl, 1, B))
    left = jnp.where(kept, jnp.where(above, jnp.where(k == z, band, straight), crossed), zero)
    left = lax.all_gather(left, "y", axis=0, tiled=True).reshape(ny, nl, B, B)

    half = with_layout_constraint(crossed.transpose(1, 0, 2).reshape(B, plane), Layout((0, 1)))
    half = lax.dynamic_slice(half, (0, w * panel), (B, panel))
    half = lax.ppermute(half, AXES, pairs(lambda a, b, c: (c, a), 0))
    tile = columns(y * plane + w * panel, panel)
    own = y * plane + w * panel + jnp.arange(panel, dtype=jnp.int32)[None, :]
    above = z * plane + offset[:, None] <= own
    kept = jnp.where(above, present[2], present[3])
    right = jnp.where(kept, jnp.where(above, tile, half), zero)
    right = jnp.broadcast_to(right[None], (nz, B, panel))
    right = lax.all_to_all(right, "z", split_axis=0, concat_axis=0, tiled=True)

    partial = product(left, right, z, ncore)
    partial = jnp.sum(lax.all_to_all(partial, "core", split_axis=0, concat_axis=0, tiled=True), axis=0)

    most = jnp.max(jnp.abs(partial))
    power = jnp.clip(jnp.ceil(jnp.log2(jnp.maximum(most, 1e-30))) - 14.0, -100.0, 100.0)
    grown = jnp.exp2(-power)
    tail = jnp.broadcast_to(power.astype(jnp.float16), (TAIL, panel))
    mine = u * nv + v
    total = 0.0
    for d in (2, 1, 3):
        chunk = lax.dynamic_index_in_dim(partial, mine ^ d, 0, keepdims=False)
        chunk = jnp.concatenate([(chunk * grown).astype(jnp.float16), tail], axis=0)
        got = lax.ppermute(chunk, ("u", "v"), [(a, a ^ d) for a in range(nu * nv)])
        total = total + got.astype(jnp.float32) * jnp.exp2(got[B : B + 1].astype(jnp.float32))
    total = total[:B] + lax.dynamic_index_in_dim(partial, mine, 0, keepdims=False)
    return total.astype(jnp.bfloat16)


def solution(mesh):
    finer = Mesh(mesh.devices.reshape(8, 8, 2, 2, 2, 2), AXES)
    return jax.shard_map(
        body,
        mesh=finer,
        in_specs=(P(("z", "u", "v", "core"), None), P()),
        out_specs=P(("z", "u", "v", "core"), ("y", "w")),
        check_vma=False,
    )
```

```python
import jax
import jax.numpy as jnp
from jax import lax
from jax.experimental import pallas as pl
from jax.experimental.pallas import tpu as pltpu
from jax.experimental.layout import Layout, with_layout_constraint
from jax.sharding import Mesh, PartitionSpec as P

B = 128
AXES = ("z", "y", "w", "u", "v", "core")
TAIL = 16


def product_kernel(at_ref, left_ref, right_ref, out_ref, ordered):
    n, depth, _ = right_ref.shape
    z = at_ref[0]

    @pl.when(pl.program_id(0) == 0)
    def _():
        for p in range(n):
            ordered[p * depth : (p + 1) * depth, :] = right_ref[lax.rem(p - z + n, n)]

    out_ref[0] = lax.dot_general(
        left_ref[:, 0].reshape(n * depth, B),
        ordered[...],
        (((0,), (0,)), ((), ())),
        preferred_element_type=jnp.float32,
    )


def product(left, right, z, core, cores):
    n, depth, panel = right.shape
    count = left.shape[1] // cores
    return pl.pallas_call(
        product_kernel,
        grid_spec=pltpu.PrefetchScalarGridSpec(
            num_scalar_prefetch=1,
            grid=(count,),
            in_specs=[
                pl.BlockSpec((n, 1, depth, B), lambda m, at: (0, m * cores + at[1], 0, 0)),
                pl.BlockSpec((n, depth, panel), lambda m, _: (0, 0, 0)),
            ],
            out_specs=pl.BlockSpec((1, B, panel), lambda m, _: (m, 0, 0)),
            scratch_shapes=[pltpu.VMEM((n * depth, panel), left.dtype)],
        ),
        out_shape=jax.ShapeDtypeStruct((count, B, panel), jnp.float32),
        compiler_params=pltpu.CompilerParams(vmem_limit_bytes=50 * 1024 * 1024),
        cost_estimate=pl.CostEstimate(
            flops=2 * n * depth * count * B * panel,
            bytes_accessed=2 * n * depth * (count * B + panel) + 4 * count * B * panel,
            transcendentals=0,
        ),
        name="product",
    )(jnp.stack([z, core]), left, right)


def body(stored, pattern):
    nz, ny, nw, nu, nv, ncore = (lax.axis_size(a) for a in AXES)
    z, y, w, u, v, core = (lax.axis_index(a) for a in AXES)
    nl = nu * nv * ncore
    l = (u * nv + v) * ncore + core
    g = z * nl + l
    plane = nl * B
    panel = plane // nw

    def columns(start, width):
        return lax.dynamic_slice(stored, (0, start), (B, width))

    def here(rows, first, count, across):
        if across:
            found = lax.dynamic_slice(pattern, (rows, first), (1, count))
        else:
            found = lax.dynamic_slice(pattern, (first, rows), (count, 1)).reshape(1, count)
        return jnp.repeat(found, B, axis=1) > 0

    def flat(zz, yy, r):
        return (zz * ny + yy) * (nw * nl) + r

    def pairs(target, least):
        found = []
        for a in range(nz):
            for b in range(ny):
                c = (b - a) % nz
                if c >= a + least:
                    found += [(flat(a, b, r), flat(*target(a, b, c), r)) for r in range(nw * nl)]
        return found

    k = lax.rem(y - z + nz, nz)
    band = columns(k * plane, plane).reshape(B, nl, B).transpose(1, 0, 2)
    straight = lax.ppermute(band, AXES, pairs(lambda a, b, c: (c, b), 1))
    turned = columns(k * plane, plane).T.reshape(nl, B, B)
    crossed = lax.all_to_all(turned, ("u", "v", "core"), split_axis=0, concat_axis=0, tiled=True)
    first = y * nl + w * (nl // nw)
    present = (
        here(k * nl + l, z * nl, nl, True),
        here(k * nl + l, z * nl, nl, False),
        here(g, first, nl // nw, True),
        here(g, first, nl // nw, False),
    )
    crossed, present = lax.optimization_barrier((crossed, present))
    zero = jnp.zeros((), stored.dtype)
    offset = l * B + jnp.arange(B, dtype=jnp.int32)
    across = jnp.arange(plane, dtype=jnp.int32).reshape(nl, 1, B)
    above = k * plane + offset[None, :, None] <= z * plane + across
    kept = jnp.where(above, present[0].reshape(nl, 1, B), present[1].reshape(nl, 1, B))
    left = jnp.where(kept, jnp.where(above, jnp.where(k == z, band, straight), crossed), zero)
    left = lax.all_gather(left, "y", axis=0, tiled=True).reshape(ny, nl, B, B)

    half = with_layout_constraint(crossed.transpose(1, 0, 2).reshape(B, plane), Layout((0, 1)))
    half = lax.dynamic_slice(half, (0, w * panel), (B, panel))
    half = lax.ppermute(half, AXES, pairs(lambda a, b, c: (c, a), 0))
    tile = columns(y * plane + w * panel, panel)
    own = y * plane + w * panel + jnp.arange(panel, dtype=jnp.int32)[None, :]
    above = z * plane + offset[:, None] <= own
    kept = jnp.where(above, present[2], present[3])
    right = jnp.where(kept, jnp.where(above, tile, half), zero)
    right = jnp.broadcast_to(right[None], (nz, B, panel))
    right = lax.all_to_all(right, "z", split_axis=0, concat_axis=0, tiled=True)

    partial = product(left, right, z, ncore - 1 - core, ncore)
    partial = lax.ppermute(partial, "core", [(a, ncore - 1 - a) for a in range(ncore)])
    partial = partial + product(left, right, z, core, ncore)

    most = jnp.max(jnp.abs(partial))
    power = jnp.clip(jnp.ceil(jnp.log2(jnp.maximum(most, 1e-30))) - 14.0, -100.0, 100.0)
    grown = jnp.exp2(-power)
    tail = jnp.broadcast_to(power.astype(jnp.float16), (TAIL, panel))
    mine = u * nv + v
    total = 0.0
    for d in (2, 1, 3):
        chunk = lax.dynamic_index_in_dim(partial, mine ^ d, 0, keepdims=False)
        chunk = jnp.concatenate([(chunk * grown).astype(jnp.float16), tail], axis=0)
        got = lax.ppermute(chunk, ("u", "v"), [(a, a ^ d) for a in range(nu * nv)])
        total = total + got.astype(jnp.float32) * jnp.exp2(got[B : B + 1].astype(jnp.float32))
    total = total[:B] + lax.dynamic_index_in_dim(partial, mine, 0, keepdims=False)
    return total.astype(jnp.bfloat16)


def solution(mesh):
    finer = Mesh(mesh.devices.reshape(8, 8, 2, 2, 2, 2), AXES)
    return jax.shard_map(
        body,
        mesh=finer,
        in_specs=(P(("z", "u", "v", "core"), None), P()),
        out_specs=P(("z", "u", "v", "core"), ("y", "w")),
        check_vma=False,
    )
```

```python
import jax
import jax.numpy as jnp
from jax import lax
from jax.experimental import pallas as pl
from jax.experimental.pallas import tpu as pltpu
from jax.experimental.layout import Layout, with_layout_constraint
from jax.sharding import Mesh, PartitionSpec as P

B = 128
AXES = ("z", "y", "w", "u", "v", "core")
TAIL = 16


def product_kernel(z_ref, left_ref, right_ref, out_ref, ordered):
    n, depth, _ = right_ref.shape
    z = z_ref[0]

    @pl.when(pl.program_id(0) == 0)
    def _():
        for p in range(n):
            ordered[p * depth : (p + 1) * depth, :] = right_ref[lax.rem(p - z + n, n)]

    for a in range(out_ref.shape[0]):
        out_ref[a, 0] = lax.dot_general(
            left_ref[:, a].reshape(n * depth, B),
            ordered[...],
            (((0,), (0,)), ((), ())),
            preferred_element_type=jnp.float32,
        )


def product(left, right, z, cores):
    n, depth, panel = right.shape
    wide = left.shape[1] * B
    step = cores * B
    return pl.pallas_call(
        product_kernel,
        grid_spec=pltpu.PrefetchScalarGridSpec(
            num_scalar_prefetch=1,
            grid=(wide // step,),
            in_specs=[
                pl.BlockSpec((n, cores, depth, B), lambda m, _: (0, m, 0, 0)),
                pl.BlockSpec((n, depth, panel), lambda m, _: (0, 0, 0)),
            ],
            out_specs=pl.BlockSpec((cores, 1, B, panel), lambda m, _: (0, m, 0, 0)),
            scratch_shapes=[pltpu.VMEM((n * depth, panel), left.dtype)],
        ),
        out_shape=jax.ShapeDtypeStruct((cores, wide // step, B, panel), jnp.float32),
        compiler_params=pltpu.CompilerParams(vmem_limit_bytes=50 * 1024 * 1024),
        cost_estimate=pl.CostEstimate(
            flops=2 * n * depth * wide * panel,
            bytes_accessed=2 * n * depth * (wide + panel) + 4 * wide * panel,
            transcendentals=0,
        ),
        name="product",
    )(z.reshape(1), left, right)


def body(stored, pattern):
    nz, ny, nw, nu, nv, ncore = (lax.axis_size(a) for a in AXES)
    z, y, w, u, v, core = (lax.axis_index(a) for a in AXES)
    nl = nu * nv * ncore
    l = (u * nv + v) * ncore + core
    g = z * nl + l
    plane = nl * B
    panel = plane // nw

    def columns(start, width):
        return lax.dynamic_slice(stored, (0, start), (B, width))

    def here(rows, first, count, across):
        if across:
            found = lax.dynamic_slice(pattern, (rows, first), (1, count))
        else:
            found = lax.dynamic_slice(pattern, (first, rows), (count, 1)).reshape(1, count)
        return jnp.repeat(found, B, axis=1) > 0

    def flat(zz, yy, r):
        return (zz * ny + yy) * (nw * nl) + r

    def pairs(target, least):
        found = []
        for a in range(nz):
            for b in range(ny):
                c = (b - a) % nz
                if c >= a + least:
                    found += [(flat(a, b, r), flat(*target(a, b, c), r)) for r in range(nw * nl)]
        return found

    k = lax.rem(y - z + nz, nz)
    band = columns(k * plane, plane).reshape(B, nl, B).transpose(1, 0, 2)
    band = lax.optimization_barrier(band)
    straight = lax.ppermute(band, AXES, pairs(lambda a, b, c: (c, b), 1))
    turned = band.transpose(0, 2, 1)
    crossed = lax.all_to_all(turned, ("u", "v", "core"), split_axis=0, concat_axis=0, tiled=True)
    first = y * nl + w * (nl // nw)
    present = (
        here(k * nl + l, z * nl, nl, True),
        here(k * nl + l, z * nl, nl, False),
        here(g, first, nl // nw, True),
        here(g, first, nl // nw, False),
    )
    crossed, present = lax.optimization_barrier((crossed, present))
    zero = jnp.zeros((), stored.dtype)
    offset = l * B + jnp.arange(B, dtype=jnp.int32)
    across = jnp.arange(plane, dtype=jnp.int32).reshape(nl, 1, B)
    above = k * plane + offset[None, :, None] <= z * plane + across
    kept = jnp.where(above, present[0].reshape(nl, 1, B), present[1].reshape(nl, 1, B))
    left = jnp.where(kept, jnp.where(above, jnp.where(k == z, band, straight), crossed), zero)
    left = lax.all_gather(left, "y", axis=0, tiled=True).reshape(ny, nl, B, B)

    half = with_layout_constraint(crossed.transpose(1, 0, 2).reshape(B, plane), Layout((0, 1)))
    half = lax.dynamic_slice(half, (0, w * panel), (B, panel))
    half = lax.ppermute(half, AXES, pairs(lambda a, b, c: (c, a), 0))
    tile = columns(y * plane + w * panel, panel)
    own = y * plane + w * panel + jnp.arange(panel, dtype=jnp.int32)[None, :]
    above = z * plane + offset[:, None] <= own
    kept = jnp.where(above, present[2], present[3])
    right = jnp.where(kept, jnp.where(above, tile, half), zero)
    right = jnp.broadcast_to(right[None], (nz, B, panel))
    right = lax.all_to_all(right, "z", split_axis=0, concat_axis=0, tiled=True)

    partial = product(left, right, z, ncore)
    partial = jnp.sum(lax.all_to_all(partial, "core", split_axis=0, concat_axis=0, tiled=True), axis=0)

    most = jnp.max(jnp.abs(partial))
    power = jnp.clip(jnp.ceil(jnp.log2(jnp.maximum(most, 1e-30))) - 14.0, -100.0, 100.0)
    grown = jnp.exp2(-power)
    tail = jnp.broadcast_to(power.astype(jnp.float16), (TAIL, panel))
    mine = u * nv + v
    total = 0.0
    for d in (2, 1, 3):
        chunk = lax.dynamic_index_in_dim(partial, mine ^ d, 0, keepdims=False)
        chunk = jnp.concatenate([(chunk * grown).astype(jnp.float16), tail], axis=0)
        got = lax.ppermute(chunk, ("u", "v"), [(a, a ^ d) for a in range(nu * nv)])
        total = total + got.astype(jnp.float32) * jnp.exp2(got[B : B + 1].astype(jnp.float32))
    total = total[:B] + lax.dynamic_index_in_dim(partial, mine, 0, keepdims=False)
    return total.astype(jnp.bfloat16)


def solution(mesh):
    finer = Mesh(mesh.devices.reshape(8, 8, 2, 2, 2, 2), AXES)
    return jax.shard_map(
        body,
        mesh=finer,
        in_specs=(P(("z", "u", "v", "core"), None), P()),
        out_specs=P(("z", "u", "v", "core"), ("y", "w")),
        check_vma=False,
    )
```
